32 devices in a mesh: grp: 2 (over y), col: 4 (over z), row: 2 (over x), dir: 2 (over core).
Axes of the slice: x: 2, y: 2, z: 4, core: 2. Of those that a mesh axis runs over, the one named last changes fastest.
Arguments:
- slopes_in: bfloat16 [512, 8192], P(None, ('grp', 'col')), parts along dimension 1, may hold values from -6 to 6
- basis_left: bfloat16 [12, 16, 256, 256], P(('row', 'dir'), 'col'), may hold values from -0.09375 to 0.09375
- basis_right: bfloat16 [12, 16, 256, 256], P(('row', 'dir'), 'col'), may hold values from -0.375 to 0.375
- rank_blocks: int32 [12, 16], P(('row', 'dir'), 'col'), may hold values from 1 to 4
- tile_owner: int32 [16], replicated, may hold values from 0 to 15, each once
- footprint: int32 [4, 4, 4, 2048], P(('row', 'dir')), may hold values from 0 to 767
- trace_weight: float32 [4, 4, 4, 2048], P(('row', 'dir')), may hold values from 0 to 0.5
- fitting: bfloat16 [2048, 4096], P(None, 'col'), may hold values from -0.125 to 0.125
Outputs:
- commands: bfloat16 [4, 1024, 4096], P(('row', 'dir'), 'grp', 'col'), parts along dimension 1
The draws below stay inside these ranges and needn't reach their ends.
There are 2 independent parts, one for each index of `grp`. The reference program is written for one: setup_inputs(seed, part) draws one part's arguments, and reference() takes and returns one part's arrays. A program takes and returns all parts, laid end to end along the dimension named above; an argument that names none is the same for every part. Nothing has to cross between parts.
Inputs may be any that keep to these rules, and one draw needn't show every extreme that they name: rank_blocks[i, k] is the number of leading blocks of 64 columns of tile (i, k) that are live. `tile_owner`: each slope block appears in exactly one tile slot. `footprint`: indices into one layer's points.
All inputs are finite; a program needn't handle non-finite values.
Results may differ from the reference program's by a relative error of at most 0.0064.
Values may be sent and summed in bfloat16 or wider, within the bound.
A program may use at most 128 MiB of HBM per device.

```python
import jax
import jax.numpy as jnp
from jax import lax

NB = 256
RB = 64
RMAX = 4
F = 512
L = 4
M = 2048
ACT = 4096
RK = 256
TR = 12
TC = 16
P_SIZE = 3072
S = 4096
G = 768
ND = 4


def touch_ends(drawn, stream_key, smallest, top_value):
    spot = [jax.random.randint(jax.random.fold_in(stream_key, axis), (), 0, length) for axis, length in enumerate(drawn.shape)]
    main_axis = drawn.shape.index(max(drawn.shape))
    neighbour = spot[:main_axis] + [(spot[main_axis] + 1) % drawn.shape[main_axis]] + spot[main_axis + 1:]
    return drawn.at[tuple(spot)].set(smallest).at[tuple(neighbour)].set(top_value)


def block_levels(own_key, dims, cuts, least, top_value):
    def one(position, parts):
        heights = jax.random.uniform(jax.random.fold_in(jax.random.fold_in(own_key, 6), position), (parts,), jnp.float32, least / len(cuts), top_value / len(cuts))
        return jnp.repeat(jnp.exp(heights), dims[position] // parts).reshape((-1,) + (1,) * (len(dims) - position - 1))

    level = one(*cuts[0])
    for cut in cuts[1:]:
        level = level * one(*cut)
    return level


def centred(rng, extent, spread, limit, split=(), held_as=jnp.bfloat16):
    entries = jax.random.normal(rng, extent, jnp.float32) * spread
    if len(split) > 0:
        entries = block_levels(rng, extent, split, -0.22, 0.18) * entries
    return jnp.clip(entries, min=-limit, max=limit).astype(held_as)


def setup_inputs(seed: int = 0, part: int = 0) -> dict:
    arg_keys = jax.random.split(jax.random.key(seed), 9)
    part_keys = jax.random.split(jax.random.fold_in(arg_keys[8], part), 9)
    return {
        "slopes_in": centred(part_keys[0], (F, S), 1.0, 6.0, ((1, 4),)),
        "basis_left": centred(arg_keys[1], (TR, TC, NB, RK), (RK * TC) ** -0.5, 0.09375, ((0, 4), (1, 4))),
        "basis_right": centred(arg_keys[2], (TR, TC, NB, RK), NB ** -0.5, 0.375, ((0, 4), (1, 4))),
        "rank_blocks": touch_ends(jax.random.randint(arg_keys[3], (TR, TC), 1, RMAX + 1), jax.random.fold_in(arg_keys[3], 1), 1, RMAX).astype(jnp.int32),
        "tile_owner": jax.random.permutation(arg_keys[4], TC).astype(jnp.int32),
        "footprint": touch_ends(jax.random.randint(arg_keys[5], (ND, L, 4, M), 0, G), jax.random.fold_in(arg_keys[5], 1), 0, G - 1).astype(jnp.int32),
        "trace_weight": jnp.clip(0.5 * jax.random.uniform(arg_keys[6], (ND, L, 4, M), jnp.float32) ** block_levels(arg_keys[6], (ND, L, 4, M), ((0, 4),), -0.2, 0.2), 0.0, 0.5),
        "fitting": centred(arg_keys[7], (M, ACT), M ** -0.5, 0.125, ((1, 4),)),
    }


def reference(slopes_in, basis_left, basis_right, rank_blocks, tile_owner, footprint, trace_weight, fitting):
    blocks = slopes_in.reshape(F, TC, NB)
    chosen = jnp.take(blocks, tile_owner.astype(jnp.int32), axis=1)
    chosen_f = chosen.astype(jnp.float32)
    columns = jnp.arange(RK, dtype=jnp.int32) // RB

    def one_row(packed):
        left, right, ranks = packed
        coeffs = jnp.einsum('fkn,knr->kfr', chosen_f, right.astype(jnp.float32))
        live = columns[None, None, :] < ranks[:, None, None]
        coeffs = jnp.where(live, coeffs, 0.0).astype(jnp.bfloat16)
        return jnp.einsum('kfr,knr->fn', coeffs.astype(jnp.float32), left.astype(jnp.float32))

    rows = lax.map(one_row, (basis_left, basis_right, rank_blocks))
    layers = jnp.transpose(rows, (1, 0, 2)).reshape(F, P_SIZE).astype(jnp.bfloat16)
    shifts = (jnp.arange(L, dtype=jnp.int32) * G)[:, None, None]

    def one_direction(packed):
        points, weights = packed
        flat = (points + shifts).reshape(-1)
        values = jnp.take(layers, flat, axis=1).astype(jnp.float32).reshape(F, L, 4, M)
        pupil = jnp.sum(values * weights[None], axis=(1, 2)).astype(jnp.bfloat16)
        return jnp.dot(pupil, fitting, preferred_element_type=jnp.float32).astype(jnp.bfloat16)

    return lax.map(one_direction, (footprint, trace_weight))
```

```python
import functools

import jax
import jax.numpy as jnp
from jax import lax
from jax.experimental import pallas as pl
from jax.experimental.pallas import tpu as pltpu
from jax.sharding import PartitionSpec as P

RB = 64
MESH = pl.DeviceIdType.MESH


def plain(
    slopes_in, basis_left, basis_right, rank_blocks, tile_owner, footprint, trace_weight, fitting
):
    frames = slopes_in.shape[0]
    tile_size = basis_left.shape[2]
    rows_here, slots_here = basis_left.shape[:2]
    rank_cols = basis_left.shape[3]
    owners = lax.dynamic_slice_in_dim(tile_owner, lax.axis_index("col") * slots_here, slots_here, 0)
    share = frames // lax.axis_size(("row", "dir"))
    mine = lax.dynamic_slice_in_dim(slopes_in, lax.axis_index(("row", "dir")) * share, share, 0)
    gathered = lax.all_gather(mine, "col", axis=1, tiled=True)
    picked = jnp.concatenate(
        [
            lax.dynamic_slice_in_dim(gathered, owners[k] * tile_size, tile_size, 1)
            for k in range(slots_here)
        ],
        axis=1,
    )
    chosen = lax.all_gather(picked, ("row", "dir"), axis=0, tiled=True)
    chosen = chosen.reshape(frames, slots_here, tile_size)
    columns = jnp.arange(rank_cols, dtype=jnp.int32) // RB
    live = columns[None, None, None, :] < rank_blocks[:, :, None, None]
    coeffs = jnp.einsum("fkn,iknr->ikfr", chosen, basis_right, preferred_element_type=jnp.float32)
    coeffs = jnp.where(live, coeffs, 0.0).astype(jnp.bfloat16)
    summed = jnp.einsum("ikfr,iknr->fin", coeffs, basis_left, preferred_element_type=jnp.float32)
    layer_block = lax.psum_scatter(
        summed.reshape(frames, rows_here * tile_size), "col", scatter_dimension=0, tiled=True
    ).astype(jnp.bfloat16)
    layers = lax.all_gather(layer_block, ("row", "dir"), axis=1, tiled=True)
    layer_count, taps, pupil_count = footprint.shape[1:]
    per_layer = layers.shape[1] // layer_count
    points = jnp.arange(per_layer, dtype=jnp.int32)[:, None]
    total = 0.0
    for l in range(layer_count):
        spread = 0.0
        for t in range(taps):
            spread += jnp.where(
                points == footprint[0, l, t][None, :], trace_weight[0, l, t][None, :], 0.0
            )
        total += jnp.dot(
            layers[:, l * per_layer : (l + 1) * per_layer],
            spread.astype(jnp.bfloat16),
            preferred_element_type=jnp.float32,
        )
    commands = jnp.dot(
        lax.all_gather(total.astype(jnp.bfloat16), "col", axis=0, tiled=True),
        fitting,
        preferred_element_type=jnp.float32,
    )
    return commands.astype(jnp.bfloat16)[None]


def fused_kernel(
    nc,
    owner_ref,
    ranks_ref,
    slopes_hbm,
    left_hbm,
    right_hbm,
    foot_ref,
    weight_ref,
    fit_hbm,
    out_ref,
    left,
    right,
    fit,
    parts,
    picks,
    chosen,
    spread,
    mixing,
    partial_sums,
    arrived,
    layers,
    load_sem,
    a1_send,
    a1_recv,
    a2_send,
    a2_recv,
    a3x_send,
    a3x_recv,
    a3c_send,
    a3c_recv,
    rs_send,
    rs_recv,
    z_send,
    z_recv,
    x_send,
    x_recv,
    c_send,
    c_recv,
):
    rows_here, slots, tile, rank_cols = left.shape
    frames = slopes_hbm.shape[0]
    quads = chosen.shape[0]
    share = frames // quads
    pieces = quads // nc
    block = frames // nc
    col, row, core = lax.axis_index("col"), lax.axis_index("row"), lax.axis_index("dir")
    here = row * 2 + core
    beside = (1 - row) * 2 + core
    sibling = {"dir": 1 - core}
    across = {"row": 1 - row}

    def ahead(j):
        return lax.rem(col + j, nc)

    def behind(j):
        return lax.rem(col + nc - j, nc)

    loads = [
        pltpu.make_async_copy(right_hbm, right, load_sem.at[0]),
        pltpu.make_async_copy(left_hbm, left, load_sem.at[1]),
        pltpu.make_async_copy(fit_hbm, fit, load_sem.at[2]),
    ]

    barrier = pltpu.get_barrier_semaphore()
    for j in range(1, nc):
        pl.semaphore_signal(barrier, inc=1, device_id={"col": ahead(j)}, device_id_type=MESH)
    for other in (sibling, across):
        pl.semaphore_signal(barrier, inc=1, device_id=other, device_id_type=MESH)
    pl.semaphore_wait(barrier, nc + 1)

    def remote(src, dst, send, recv, target):
        return pltpu.make_async_remote_copy(
            src_ref=src,
            dst_ref=dst,
            send_sem=send,
            recv_sem=recv,
            device_id=target,
            device_id_type=MESH,
        )

    sent = []
    for j in range(1, nc):
        start = pl.multiple_of((ahead(j) * pieces + here) * share, share)
        for b in range(slots):
            copy = remote(
                slopes_hbm.at[pl.ds(start, share), pl.ds(b * tile, tile)],
                parts.at[col * slots + b],
                a1_send.at[(j - 1) * slots + b],
                a1_recv.at[(j - 1) * slots + b],
                {"col": ahead(j)},
            )
            copy.start()
            sent.append(copy)
    first = sent
    start = pl.multiple_of((col * pieces + here) * share, share)
    own = []
    for b in range(slots):
        copy = pltpu.make_async_copy(
            slopes_hbm.at[pl.ds(start, share), pl.ds(b * tile, tile)],
            parts.at[col * slots + b],
            load_sem.at[3 + b],
        )
        copy.start()
        own.append(copy)
    for copy in loads:
        copy.start()
    loads[2].wait()

    layer_count, taps, pupil_count = foot_ref.shape[1:]
    points = mixing.shape[0]
    per_layer = points // layer_count
    step = spread.shape[0]
    per_step = per_layer // step
    steps = points // step
    wide = 256

    def mix(n, carry):
        l, base = n // per_step, (n % per_step) * step
        at = lax.broadcasted_iota(jnp.int32, (step, wide), 0) + base
        for m in range(0, pupil_count, wide):
            total = jnp.zeros((step, wide), jnp.float32)
            for t in range(taps):
                total += jnp.where(
                    at == foot_ref[0, l, t : t + 1, m : m + wide],
                    weight_ref[0, l, t : t + 1, m : m + wide],
                    0.0,
                )
            spread[:, m : m + wide] = total.astype(jnp.bfloat16)
        mixing[pl.ds(pl.multiple_of(n * step, step), step), :] = jnp.dot(
            spread[...], fit[...], preferred_element_type=jnp.float32
        ).astype(jnp.bfloat16)
        return carry

    cuts = [0, steps // 4, steps // 2, steps]
    lax.fori_loop(cuts[0], cuts[1], mix, 0)

    for copy in own:
        copy.wait()
    for copy in first:
        copy.wait_recv()
    second = []
    for j in range(nc):
        for k in range(slots):
            picks[ahead(j), k] = parts[owner_ref[ahead(j) * slots + k]]
        if j:
            copy = remote(
                picks.at[ahead(j)],
                chosen.at[col * pieces + here],
                a2_send.at[j - 1],
                a2_recv.at[j - 1],
                {"col": ahead(j)},
            )
            copy.start()
            second.append(copy)
    chosen[col * pieces + here] = picks[col]

    third = []

    def spread_share(j):
        at = behind(j) * pieces + here
        for send, recv, target in (
            (a3x_send.at[j], a3x_recv.at[j], across),
            (a3c_send.at[j], a3c_recv.at[j], sibling),
        ):
            copy = remote(chosen.at[at], chosen.at[at], send, recv, target)
            copy.start()
            third.append(copy)

    spread_share(0)
    lax.fori_loop(cuts[1], cuts[2], mix, 0)
    for j in range(1, nc):
        second[j - 1].wait_recv()
        spread_share(j)
    fourth = []
    for j in range(nc):
        third[2 * j].wait_recv()
        at = behind(j) * pieces + beside
        copy = remote(
            chosen.at[at], chosen.at[at], a3c_send.at[nc + j], a3c_recv.at[nc + j], sibling
        )
        copy.start()
        fourth.append(copy)
    for j in range(nc):
        third[2 * j + 1].wait_recv()
        fourth[j].wait_recv()
    loads[0].wait()
    loads[1].wait()

    lane = lax.broadcasted_iota(jnp.int32, (1, rank_cols), 1)
    sums = []
    for i in range(rows_here):
        total = jnp.zeros((frames, tile), jnp.float32)
        for k in range(slots):
            coeffs = jnp.dot(
                chosen[:, k].reshape(frames, tile), right[i, k], preferred_element_type=jnp.float32
            )
            coeffs = jnp.where(lane < ranks_ref[i, k] * RB, coeffs, 0.0).astype(jnp.bfloat16)
            total += lax.dot_general(
                coeffs, left[i, k], (((1,), (1,)), ((), ())), preferred_element_type=jnp.float32
            )
        partial_sums[i] = total.astype(jnp.bfloat16).reshape(nc, block, tile)
        for j in range(1, nc):
            copy = remote(
                partial_sums.at[i, ahead(j)],
                arrived.at[j - 1, i],
                rs_send.at[(j - 1) * rows_here + i],
                rs_recv.at[(j - 1) * rows_here + i],
                {"col": ahead(j)},
            )
            copy.start()
            sums.append(copy)
    lax.fori_loop(cuts[2], cuts[3], mix, 0)
    for copy in sums:
        copy.wait_recv()
    for i in range(rows_here):
        total = partial_sums[i, col].astype(jnp.float32)
        for j in range(1, nc):
            total += arrived[j - 1, i].astype(jnp.float32)
        layers[here, col, :, i * tile : (i + 1) * tile] = total.astype(jnp.bfloat16)

    along = []
    for j in range(1, nc):
        at = layers.at[here, col]
        copy = remote(at, at, z_send.at[j - 1], z_recv.at[j - 1], {"col": ahead(j)})
        copy.start()
        along.append(copy)
    over, within = [], []

    def spread_layers(j):
        at = layers.at[here, behind(j)]
        copy = remote(at, at, x_send.at[j], x_recv.at[j], across)
        copy.start()
        over.append(copy)
        copy = remote(at, at, c_send.at[j], c_recv.at[j], sibling)
        copy.start()
        within.append(copy)

    spread_layers(0)
    for j in range(1, nc):
        along[j - 1].wait_recv()
        spread_layers(j)
    passed = []
    for j in range(nc):
        over[j].wait_recv()
        at = layers.at[beside, behind(j)]
        copy = remote(at, at, c_send.at[nc + j], c_recv.at[nc + j], sibling)
        copy.start()
        passed.append(copy)
    for j in range(nc):
        within[j].wait_recv()
        passed[j].wait_recv()
    depth = layers.shape[3]
    total = jnp.zeros(out_ref.shape[1:], jnp.float32)
    for r in range(pieces):
        total += jnp.dot(
            layers[r].reshape(frames, depth),
            mixing[r * depth : (r + 1) * depth, :],
            preferred_element_type=jnp.float32,
        )
    out_ref[0] = total.astype(jnp.bfloat16)
    for copy in first + second + third + fourth + sums + along + over + within + passed:
        copy.wait_send()


def fused(
    nc, slopes_in, basis_left, basis_right, rank_blocks, tile_owner, footprint, trace_weight, fitting
):
    frames = slopes_in.shape[0]
    rows_here, slots, tile, rank_cols = basis_left.shape
    pieces = 4
    share = frames // (nc * pieces)
    points = rows_here * tile * pieces
    pupil_count, acts = fitting.shape
    step = tile
    bf16 = jnp.bfloat16
    dma = pltpu.SemaphoreType.DMA
    anywhere = pl.BlockSpec(memory_space=pl.ANY)
    smem = pl.BlockSpec(memory_space=pltpu.SMEM)
    vmem = pl.BlockSpec(memory_space=pltpu.VMEM)
    return pl.pallas_call(
        functools.partial(fused_kernel, nc),
        out_shape=jax.ShapeDtypeStruct((1, frames, acts), bf16),
        in_specs=[smem, smem, anywhere, anywhere, anywhere, vmem, vmem, anywhere],
        out_specs=vmem,
        scratch_shapes=[
            pltpu.VMEM(basis_left.shape, bf16),
            pltpu.VMEM(basis_right.shape, bf16),
            pltpu.VMEM(fitting.shape, bf16),
            pltpu.VMEM((nc * slots, share, tile), bf16),
            pltpu.VMEM((nc, slots, share, tile), bf16),
            pltpu.VMEM((nc * pieces, slots, share, tile), bf16),
            pltpu.VMEM((step, pupil_count), bf16),
            pltpu.VMEM((points, acts), bf16),
            pltpu.VMEM((rows_here, nc, frames // nc, tile), bf16),
            pltpu.VMEM((nc - 1, rows_here, frames // nc, tile), bf16),
            pltpu.VMEM((pieces, nc, frames // nc, rows_here * tile), bf16),
            dma((3 + slots,)),
            dma(((nc - 1) * slots,)),
            dma(((nc - 1) * slots,)),
            dma((nc - 1,)),
            dma((nc - 1,)),
            dma((nc,)),
            dma((nc,)),
            dma((2 * nc,)),
            dma((2 * nc,)),
            dma(((nc - 1) * rows_here,)),
            dma(((nc - 1) * rows_here,)),
            dma((nc - 1,)),
            dma((nc - 1,)),
            dma((nc,)),
            dma((nc,)),
            dma((2 * nc,)),
            dma((2 * nc,)),
        ],
        compiler_params=pltpu.CompilerParams(
            collective_id=0, has_side_effects=True, vmem_limit_bytes=52 * 2**20
        ),
    )(
        tile_owner,
        rank_blocks,
        slopes_in,
        basis_left,
        basis_right,
        footprint,
        trace_weight,
        fitting,
    )


def solution(mesh):
    placed = (
        P(None, ("grp", "col")),
        P(("row", "dir"), "col", None, None),
        P(("row", "dir"), "col", None, None),
        P(("row", "dir"), "col"),
        P(),
        P(("row", "dir"), None, None, None),
        P(("row", "dir"), None, None, None),
        P(None, "col"),
    )

    def shards(slopes_in, basis_left, basis_right, rank_blocks, tile_owner, footprint, *rest):
        nc = mesh.shape["col"]
        pieces = mesh.shape["row"] * mesh.shape["dir"]
        tile = basis_left.shape[2]
        per_layer = basis_left.shape[0] * pieces * tile // footprint.shape[1]
        fits = (
            mesh.shape["row"] == 2
            and mesh.shape["dir"] == 2
            and nc > 1
            and slopes_in.shape[0] % (nc * pieces * 16) == 0
            and slopes_in.shape[1] == basis_left.shape[1] * tile
            and per_layer % tile == 0
        )
        body = functools.partial(fused, nc) if fits else plain
        return body(
            slopes_in, basis_left, basis_right, rank_blocks, tile_owner, footprint, *rest
        )

    return jax.shard_map(
        shards,
        mesh=mesh,
        in_specs=placed,
        out_specs=P(("row", "dir"), "grp", "col"),
        check_vma=False,
    )
```

```python
import functools

import jax
import jax.numpy as jnp
from jax import lax
from jax.experimental import pallas as pl
from jax.experimental.pallas import tpu as pltpu
from jax.sharding import PartitionSpec as P

RB = 64
MESH = pl.DeviceIdType.MESH


def plain(
    slopes_in, basis_left, basis_right, rank_blocks, tile_owner, footprint, trace_weight, fitting
):
    frames = slopes_in.shape[0]
    tile_size = basis_left.shape[2]
    rows_here, slots_here = basis_left.shape[:2]
    rank_cols = basis_left.shape[3]
    owners = lax.dynamic_slice_in_dim(tile_owner, lax.axis_index("col") * slots_here, slots_here, 0)
    share = frames // lax.axis_size(("row", "dir"))
    mine = lax.dynamic_slice_in_dim(slopes_in, lax.axis_index(("row", "dir")) * share, share, 0)
    gathered = lax.all_gather(mine, "col", axis=1, tiled=True)
    picked = jnp.concatenate(
        [
            lax.dynamic_slice_in_dim(gathered, owners[k] * tile_size, tile_size, 1)
            for k in range(slots_here)
        ],
        axis=1,
    )
    chosen = lax.all_gather(picked, ("row", "dir"), axis=0, tiled=True)
    chosen = chosen.reshape(frames, slots_here, tile_size)
    columns = jnp.arange(rank_cols, dtype=jnp.int32) // RB
    live = columns[None, None, None, :] < rank_blocks[:, :, None, None]
    coeffs = jnp.einsum("fkn,iknr->ikfr", chosen, basis_right, preferred_element_type=jnp.float32)
    coeffs = jnp.where(live, coeffs, 0.0).astype(jnp.bfloat16)
    summed = jnp.einsum("ikfr,iknr->fin", coeffs, basis_left, preferred_element_type=jnp.float32)
    layer_block = lax.psum_scatter(
        summed.reshape(frames, rows_here * tile_size), "col", scatter_dimension=0, tiled=True
    ).astype(jnp.bfloat16)
    layers = lax.all_gather(layer_block, ("row", "dir"), axis=1, tiled=True)
    layer_count, taps, pupil_count = footprint.shape[1:]
    per_layer = layers.shape[1] // layer_count
    points = jnp.arange(per_layer, dtype=jnp.int32)[:, None]
    total = 0.0
    for l in range(layer_count):
        spread = 0.0
        for t in range(taps):
            spread += jnp.where(
                points == footprint[0, l, t][None, :], trace_weight[0, l, t][None, :], 0.0
            )
        total += jnp.dot(
            layers[:, l * per_layer : (l + 1) * per_layer],
            spread.astype(jnp.bfloat16),
            preferred_element_type=jnp.float32,
        )
    commands = jnp.dot(
        lax.all_gather(total.astype(jnp.bfloat16), "col", axis=0, tiled=True),
        fitting,
        preferred_element_type=jnp.float32,
    )
    return commands.astype(jnp.bfloat16)[None]


def fused_kernel(
    nc,
    owner_ref,
    ranks_ref,
    slopes_hbm,
    left_hbm,
    right_hbm,
    foot_hbm,
    weight_hbm,
    fit_hbm,
    out_ref,
    foot_ref,
    weight_ref,
    left,
    right,
    fit,
    parts,
    picks,
    chosen,
    spread,
    mixing,
    partial_sums,
    arrived,
    layers,
    load_sem,
    a1_send,
    a1_recv,
    a2_send,
    a2_recv,
    a3x_send,
    a3x_recv,
    a3c_send,
    a3c_recv,
    rs_send,
    rs_recv,
    z_send,
    z_recv,
    x_send,
    x_recv,
    c_send,
    c_recv,
):
    rows_here, slots, tile, rank_cols = left.shape
    frames = slopes_hbm.shape[0]
    quads = chosen.shape[0]
    share = frames // quads
    pieces = quads // nc
    block = frames // nc
    col, row, core = lax.axis_index("col"), lax.axis_index("row"), lax.axis_index("dir")
    here = row * 2 + core
    beside = (1 - row) * 2 + core
    sibling = {"dir": 1 - core}
    across = {"row": 1 - row}

    def ahead(j):
        return lax.rem(col + j, nc)

    def behind(j):
        return lax.rem(col + nc - j, nc)

    loads = [
        pltpu.make_async_copy(foot_hbm, foot_ref, load_sem.at[0]),
        pltpu.make_async_copy(weight_hbm, weight_ref, load_sem.at[1]),
        pltpu.make_async_copy(fit_hbm, fit, load_sem.at[2]),
        pltpu.make_async_copy(right_hbm, right, load_sem.at[3]),
        pltpu.make_async_copy(left_hbm, left, load_sem.at[4]),
    ]
    for copy in loads:
        copy.start()

    barrier = pltpu.get_barrier_semaphore()
    for j in range(1, nc):
        pl.semaphore_signal(barrier, inc=1, device_id={"col": ahead(j)}, device_id_type=MESH)
    for other in (sibling, across):
        pl.semaphore_signal(barrier, inc=1, device_id=other, device_id_type=MESH)
    pl.semaphore_wait(barrier, nc + 1)

    def remote(src, dst, send, recv, target):
        return pltpu.make_async_remote_copy(
            src_ref=src,
            dst_ref=dst,
            send_sem=send,
            recv_sem=recv,
            device_id=target,
            device_id_type=MESH,
        )

    sent = []
    for j in range(1, nc):
        start = pl.multiple_of((ahead(j) * pieces + here) * share, share)
        for b in range(slots):
            copy = remote(
                slopes_hbm.at[pl.ds(start, share), pl.ds(b * tile, tile)],
                parts.at[col * slots + b],
                a1_send.at[(j - 1) * slots + b],
                a1_recv.at[(j - 1) * slots + b],
                {"col": ahead(j)},
            )
            copy.start()
            sent.append(copy)
    first = sent
    start = pl.multiple_of((col * pieces + here) * share, share)
    own = []
    for b in range(slots):
        copy = pltpu.make_async_copy(
            slopes_hbm.at[pl.ds(start, share), pl.ds(b * tile, tile)],
            parts.at[col * slots + b],
            load_sem.at[5 + b],
        )
        copy.start()
        own.append(copy)
    for copy in loads[:3]:
        copy.wait()

    layer_count, taps, pupil_count = foot_ref.shape[1:]
    points = mixing.shape[0]
    per_layer = points // layer_count
    step = spread.shape[0]
    per_step = per_layer // step
    steps = points // step
    wide = 256

    def mix(n, carry):
        l, base = n // per_step, (n % per_step) * step
        at = lax.broadcasted_iota(jnp.int32, (step, wide), 0) + base
        for m in range(0, pupil_count, wide):
            total = jnp.zeros((step, wide), jnp.float32)
            for t in range(taps):
                total += jnp.where(
                    at == foot_ref[0, l, t : t + 1, m : m + wide],
                    weight_ref[0, l, t : t + 1, m : m + wide],
                    0.0,
                )
            spread[:, m : m + wide] = total.astype(jnp.bfloat16)
        mixing[pl.ds(pl.multiple_of(n * step, step), step), :] = jnp.dot(
            spread[...], fit[...], preferred_element_type=jnp.float32
        ).astype(jnp.bfloat16)
        return carry

    cuts = [0, steps // 4, steps // 2]
    lax.fori_loop(cuts[0], cuts[1], mix, 0)

    for copy in own:
        copy.wait()
    for copy in first:
        copy.wait_recv()
    second = []
    for j in range(nc):
        for k in range(slots):
            picks[ahead(j), k] = parts[owner_ref[ahead(j) * slots + k]]
        if j:
            copy = remote(
                picks.at[ahead(j)],
                chosen.at[col * pieces + here],
                a2_send.at[j - 1],
                a2_recv.at[j - 1],
                {"col": ahead(j)},
            )
            copy.start()
            second.append(copy)
    chosen[col * pieces + here] = picks[col]

    third = []

    def spread_share(j):
        at = behind(j) * pieces + here
        for send, recv, target in (
            (a3x_send.at[j], a3x_recv.at[j], across),
            (a3c_send.at[j], a3c_recv.at[j], sibling),
        ):
            copy = remote(chosen.at[at], chosen.at[at], send, recv, target)
            copy.start()
            third.append(copy)

    spread_share(0)
    lax.fori_loop(cuts[1], cuts[2], mix, 0)
    for j in range(1, nc):
        second[j - 1].wait_recv()
        spread_share(j)
    fourth = []
    for j in range(nc):
        third[2 * j].wait_recv()
        at = behind(j) * pieces + beside
        copy = remote(
            chosen.at[at], chosen.at[at], a3c_send.at[nc + j], a3c_recv.at[nc + j], sibling
        )
        copy.start()
        fourth.append(copy)
    for j in range(nc):
        third[2 * j + 1].wait_recv()
        fourth[j].wait_recv()
    loads[3].wait()
    loads[4].wait()

    lane = lax.broadcasted_iota(jnp.int32, (1, rank_cols), 1)
    sums = []
    for i in range(rows_here):
        total = jnp.zeros((frames, tile), jnp.float32)
        for k in range(slots):
            coeffs = jnp.dot(
                chosen[:, k].reshape(frames, tile), right[i, k], preferred_element_type=jnp.float32
            )
            coeffs = jnp.where(lane < ranks_ref[i, k] * RB, coeffs, 0.0).astype(jnp.bfloat16)
            total += lax.dot_general(
                coeffs, left[i, k], (((1,), (1,)), ((), ())), preferred_element_type=jnp.float32
            )
        partial_sums[i] = total.astype(jnp.bfloat16).reshape(nc, block, tile)
        for j in range(1, nc):
            copy = remote(
                partial_sums.at[i, ahead(j)],
                arrived.at[j - 1, i],
                rs_send.at[(j - 1) * rows_here + i],
                rs_recv.at[(j - 1) * rows_here + i],
                {"col": ahead(j)},
            )
            copy.start()
            sums.append(copy)
    marks = [steps * 2 // 3 + (steps - steps * 2 // 3) * n // rows_here for n in range(rows_here + 1)]
    lax.fori_loop(cuts[2], marks[0], mix, 0)
    relayed = []

    def piece(r, b, i):
        return layers.at[r, b, :, pl.ds(i * tile, tile)]

    def pass_on(cond, r, b, i, send, recv, target):
        copy = remote(piece(r, b, i), piece(r, b, i), send, recv, target)
        if cond is None:
            copy.start()
        else:
            pl.when(cond)(copy.start)
        relayed.append((cond, copy))

    def both(x, y):
        return y if x is None else jnp.logical_and(x, y)

    def hand_out(cond, s, up, i):
        b = col - s if up else col + s
        if s < nc - 1:
            for way in (True, False) if s == 0 else (up,):
                n = (s * 2 + way) * rows_here + i
                more = both(cond, col < nc - 1 if way else col > 0)
                target = {"col": lax.rem(col + (1 if way else nc - 1), nc)}
                pass_on(more, here, b, i, z_send.at[n], z_recv.at[n], target)
        n = (s * 2 + up) * rows_here + i
        pass_on(cond, here, b, i, x_send.at[n], x_recv.at[n], across)
        pass_on(cond, here, b, i, c_send.at[0, n], c_recv.at[0, n], sibling)

    def await_recv(cond, r, b, i, send, recv):
        copy = remote(piece(r, b, i), piece(r, b, i), send, recv, sibling)
        if cond is None:
            copy.wait_recv()
        else:
            pl.when(cond)(copy.wait_recv)

    def valid(s, up):
        return None if s == 0 else (col >= s if up else col < nc - s)

    def take_z(s, up, i):
        n = ((s - 1) * 2 + up) * rows_here + i
        b = col - s if up else col + s
        await_recv(valid(s, up), here, b, i, z_send.at[n], z_recv.at[n])
        hand_out(valid(s, up), s, up, i)

    def take_x(s, up, i):
        n = (s * 2 + up) * rows_here + i
        b = col - s if up else col + s
        await_recv(valid(s, up), beside, b, i, x_send.at[n], x_recv.at[n])
        pass_on(valid(s, up), beside, b, i, c_send.at[1, n], c_recv.at[1, n], sibling)

    def ways(s):
        return (True,) if s == 0 else (True, False)

    for i in range(rows_here):
        for j in range(1, nc):
            sums[i * (nc - 1) + j - 1].wait_recv()
        total = partial_sums[i, col].astype(jnp.float32)
        for j in range(1, nc):
            total += arrived[j - 1, i].astype(jnp.float32)
        layers[here, col, :, i * tile : (i + 1) * tile] = total.astype(jnp.bfloat16)
        hand_out(None, 0, True, i)
        if i < rows_here - 1:
            lax.fori_loop(marks[i], marks[i + 1], mix, 0)
    lax.fori_loop(marks[rows_here - 1], marks[rows_here], mix, 0)
    for s in range(1, nc):
        for i in range(rows_here):
            for up in ways(s):
                take_z(s, up, i)
            for up in ways(s - 1):
                take_x(s - 1, up, i)
    for i in range(rows_here):
        for up in ways(nc - 1):
            take_x(nc - 1, up, i)
    other = row * 2 + 1 - core
    other_beside = (1 - row) * 2 + 1 - core
    for s in range(nc):
        for i in range(rows_here):
            for up in ways(s):
                n = (s * 2 + up) * rows_here + i
                b = col - s if up else col + s
                await_recv(valid(s, up), other, b, i, c_send.at[0, n], c_recv.at[0, n])
                await_recv(valid(s, up), other_beside, b, i, c_send.at[1, n], c_recv.at[1, n])
    depth = layers.shape[3]
    total = jnp.zeros(out_ref.shape[1:], jnp.float32)
    for r in range(pieces):
        total += jnp.dot(
            layers[r].reshape(frames, depth),
            mixing[r * depth : (r + 1) * depth, :],
            preferred_element_type=jnp.float32,
        )
    out_ref[0] = total.astype(jnp.bfloat16)
    for copy in first + second + third + fourth + sums:
        copy.wait_send()
    for cond, copy in relayed:
        if cond is None:
            copy.wait_send()
        else:
            pl.when(cond)(copy.wait_send)


def fused(
    nc, slopes_in, basis_left, basis_right, rank_blocks, tile_owner, footprint, trace_weight, fitting
):
    frames = slopes_in.shape[0]
    rows_here, slots, tile, rank_cols = basis_left.shape
    pieces = 4
    share = frames // (nc * pieces)
    points = rows_here * tile * pieces
    pupil_count, acts = fitting.shape
    step = tile
    bf16 = jnp.bfloat16
    dma = pltpu.SemaphoreType.DMA
    anywhere = pl.BlockSpec(memory_space=pl.ANY)
    smem = pl.BlockSpec(memory_space=pltpu.SMEM)
    vmem = pl.BlockSpec(memory_space=pltpu.VMEM)
    return pl.pallas_call(
        functools.partial(fused_kernel, nc),
        out_shape=jax.ShapeDtypeStruct((1, frames, acts), bf16),
        in_specs=[smem, smem] + [anywhere] * 6,
        out_specs=vmem,
        scratch_shapes=[
            pltpu.VMEM(footprint.shape, jnp.int32),
            pltpu.VMEM(trace_weight.shape, jnp.float32),
            pltpu.VMEM(basis_left.shape, bf16),
            pltpu.VMEM(basis_right.shape, bf16),
            pltpu.VMEM(fitting.shape, bf16),
            pltpu.VMEM((nc * slots, share, tile), bf16),
            pltpu.VMEM((nc, slots, share, tile), bf16),
            pltpu.VMEM((nc * pieces, slots, share, tile), bf16),
            pltpu.VMEM((step, pupil_count), bf16),
            pltpu.VMEM((points, acts), bf16),
            pltpu.VMEM((rows_here, nc, frames // nc, tile), bf16),
            pltpu.VMEM((nc - 1, rows_here, frames // nc, tile), bf16),
            pltpu.VMEM((pieces, nc, frames // nc, rows_here * tile), bf16),
            dma((5 + slots,)),
            dma(((nc - 1) * slots,)),
            dma(((nc - 1) * slots,)),
            dma((nc - 1,)),
            dma((nc - 1,)),
            dma((nc,)),
            dma((nc,)),
            dma((2 * nc,)),
            dma((2 * nc,)),
            dma(((nc - 1) * rows_here,)),
            dma(((nc - 1) * rows_here,)),
            dma((2 * nc * rows_here,)),
            dma((2 * nc * rows_here,)),
            dma((2 * nc * rows_here,)),
            dma((2 * nc * rows_here,)),
            dma((2, 2 * nc * rows_here)),
            dma((2, 2 * nc * rows_here)),
        ],
        compiler_params=pltpu.CompilerParams(
            collective_id=0, has_side_effects=True, vmem_limit_bytes=52 * 2**20
        ),
    )(
        tile_owner,
        rank_blocks,
        slopes_in,
        basis_left,
        basis_right,
        footprint,
        trace_weight,
        fitting,
    )


def solution(mesh):
    placed = (
        P(None, ("grp", "col")),
        P(("row", "dir"), "col", None, None),
        P(("row", "dir"), "col", None, None),
        P(("row", "dir"), "col"),
        P(),
        P(("row", "dir"), None, None, None),
        P(("row", "dir"), None, None, None),
        P(None, "col"),
    )

    def shards(slopes_in, basis_left, basis_right, rank_blocks, tile_owner, footprint, *rest):
        nc = mesh.shape["col"]
        pieces = mesh.shape["row"] * mesh.shape["dir"]
        tile = basis_left.shape[2]
        per_layer = basis_left.shape[0] * pieces * tile // footprint.shape[1]
        fits = (
            mesh.shape["row"] == 2
            and mesh.shape["dir"] == 2
            and nc > 1
            and slopes_in.shape[0] % (nc * pieces * 16) == 0
            and slopes_in.shape[1] == basis_left.shape[1] * tile
            and per_layer % tile == 0
        )
        body = functools.partial(fused, nc) if fits else plain
        return body(
            slopes_in, basis_left, basis_right, rank_blocks, tile_owner, footprint, *rest
        )

    return jax.shard_map(
        shards,
        mesh=mesh,
        in_specs=placed,
        out_specs=P(("row", "dir"), "grp", "col"),
        check_vma=False,
    )
```

```python
import functools

import jax
import jax.numpy as jnp
from jax import lax
from jax.experimental import pallas as pl
from jax.experimental.pallas import tpu as pltpu
from jax.sharding import PartitionSpec as P

RB = 64
MESH = pl.DeviceIdType.MESH


def plain(
    slopes_in, basis_left, basis_right, rank_blocks, tile_owner, footprint, trace_weight, fitting
):
    frames = slopes_in.shape[0]
    tile_size = basis_left.shape[2]
    rows_here, slots_here = basis_left.shape[:2]
    rank_cols = basis_left.shape[3]
    owners = lax.dynamic_slice_in_dim(tile_owner, lax.axis_index("col") * slots_here, slots_here, 0)
    share = frames // lax.axis_size(("row", "dir"))
    mine = lax.dynamic_slice_in_dim(slopes_in, lax.axis_index(("row", "dir")) * share, share, 0)
    gathered = lax.all_gather(mine, "col", axis=1, tiled=True)
    picked = jnp.concatenate(
        [
            lax.dynamic_slice_in_dim(gathered, owners[k] * tile_size, tile_size, 1)
            for k in range(slots_here)
        ],
        axis=1,
    )
    chosen = lax.all_gather(picked, ("row", "dir"), axis=0, tiled=True)
    chosen = chosen.reshape(frames, slots_here, tile_size)
    columns = jnp.arange(rank_cols, dtype=jnp.int32) // RB
    live = columns[None, None, None, :] < rank_blocks[:, :, None, None]
    coeffs = jnp.einsum("fkn,iknr->ikfr", chosen, basis_right, preferred_element_type=jnp.float32)
    coeffs = jnp.where(live, coeffs, 0.0).astype(jnp.bfloat16)
    summed = jnp.einsum("ikfr,iknr->fin", coeffs, basis_left, preferred_element_type=jnp.float32)
    layer_block = lax.psum_scatter(
        summed.reshape(frames, rows_here * tile_size), "col", scatter_dimension=0, tiled=True
    ).astype(jnp.bfloat16)
    layers = lax.all_gather(layer_block, ("row", "dir"), axis=1, tiled=True)
    layer_count, taps, pupil_count = footprint.shape[1:]
    per_layer = layers.shape[1] // layer_count
    points = jnp.arange(per_layer, dtype=jnp.int32)[:, None]
    total = 0.0
    for l in range(layer_count):
        spread = 0.0
        for t in range(taps):
            spread += jnp.where(
                points == footprint[0, l, t][None, :], trace_weight[0, l, t][None, :], 0.0
            )
        total += jnp.dot(
            layers[:, l * per_layer : (l + 1) * per_layer],
            spread.astype(jnp.bfloat16),
            preferred_element_type=jnp.float32,
        )
    commands = jnp.dot(
        lax.all_gather(total.astype(jnp.bfloat16), "col", axis=0, tiled=True),
        fitting,
        preferred_element_type=jnp.float32,
    )
    return commands.astype(jnp.bfloat16)[None]


def fused_kernel(
    nc,
    owner_ref,
    ranks_ref,
    slopes_hbm,
    left_hbm,
    right_hbm,
    foot_hbm,
    weight_hbm,
    fit_hbm,
    out_ref,
    foot_ref,
    weight_ref,
    left,
    right,
    fit,
    parts_a,
    parts_b,
    picks,
    chosen,
    spread,
    mixing,
    partial_sums,
    arrived,
    layers,
    load_sem,
    a1_send,
    a1_recv,
    a2_send,
    a2_recv,
    a3x_send,
    a3x_recv,
    a3c_send,
    a3c_recv,
    rs_send,
    rs_recv,
    z_send,
    z_recv,
    x_send,
    x_recv,
    c_send,
    c_recv,
):
    parts = (parts_a, parts_b)
    rows_here, slots, tile, rank_cols = left.shape
    frames = slopes_hbm.shape[0]
    halves, quads = chosen.shape[:2]
    part = frames // halves
    share = part // quads
    pieces = quads // nc
    block = part // nc
    col, row, core = lax.axis_index("col"), lax.axis_index("row"), lax.axis_index("dir")
    here = row * 2 + core
    beside = (1 - row) * 2 + core
    sibling = {"dir": 1 - core}
    across = {"row": 1 - row}

    def ahead(j):
        return lax.rem(col + j, nc)

    def behind(j):
        return lax.rem(col + nc - j, nc)

    loads = [
        pltpu.make_async_copy(foot_hbm, foot_ref, load_sem.at[0]),
        pltpu.make_async_copy(weight_hbm, weight_ref, load_sem.at[1]),
        pltpu.make_async_copy(fit_hbm, fit, load_sem.at[2]),
        pltpu.make_async_copy(right_hbm, right, load_sem.at[3]),
        pltpu.make_async_copy(left_hbm, left, load_sem.at[4]),
    ]
    for copy in loads:
        copy.start()

    barrier = pltpu.get_barrier_semaphore()
    for j in range(1, nc):
        pl.semaphore_signal(barrier, inc=1, device_id={"col": ahead(j)}, device_id_type=MESH)
    for other in (sibling, across):
        pl.semaphore_signal(barrier, inc=1, device_id=other, device_id_type=MESH)
    pl.semaphore_wait(barrier, nc + 1)

    def remote(src, dst, send, recv, target):
        return pltpu.make_async_remote_copy(
            src_ref=src,
            dst_ref=dst,
            send_sem=send,
            recv_sem=recv,
            device_id=target,
            device_id_type=MESH,
        )

    def mine(h, c, k):
        start = pl.multiple_of(h * part + (c * pieces + here) * share, share)
        return slopes_hbm.at[pl.ds(start, share), pl.ds(k * tile, tile)]

    first = []
    own = []
    for h in range(halves):
        for j in range(1, nc):
            for k in range(slots):
                copy = remote(
                    mine(h, ahead(j), k),
                    parts[h].at[col * slots + k],
                    a1_send.at[h, (j - 1) * slots + k],
                    a1_recv.at[h, (j - 1) * slots + k],
                    {"col": ahead(j)},
                )
                copy.start()
                first.append(copy)
        for k in range(slots):
            copy = pltpu.make_async_copy(
                mine(h, col, k), parts[h].at[col * slots + k], load_sem.at[5 + h * slots + k]
            )
            copy.start()
            own.append(copy)
    for copy in loads[:3]:
        copy.wait()

    layer_count, taps, pupil_count = foot_ref.shape[1:]
    points = mixing.shape[0]
    per_layer = points // layer_count
    step = spread.shape[0]
    per_step = per_layer // step
    steps = points // step
    wide = 256

    def mix(n, carry):
        l, base = n // per_step, (n % per_step) * step
        at = lax.broadcasted_iota(jnp.int32, (step, wide), 0) + base
        for m in range(0, pupil_count, wide):
            total = jnp.zeros((step, wide), jnp.float32)
            for t in range(taps):
                total += jnp.where(
                    at == foot_ref[0, l, t : t + 1, m : m + wide],
                    weight_ref[0, l, t : t + 1, m : m + wide],
                    0.0,
                )
            spread[:, m : m + wide] = total.astype(jnp.bfloat16)
        mixing[pl.ds(pl.multiple_of(n * step, step), step), :] = jnp.dot(
            spread[...], fit[...], preferred_element_type=jnp.float32
        ).astype(jnp.bfloat16)
        return carry

    cuts = [steps * n // 12 for n in (0, 3, 5, 9, 11, 12)]

    def mix_part(n):
        lax.fori_loop(cuts[n], cuts[n + 1], mix, 0)

    mix_part(0)

    second = []
    for h in range(halves):
        for copy in own[h * slots : (h + 1) * slots]:
            copy.wait()
        for copy in first[h * (nc - 1) * slots : (h + 1) * (nc - 1) * slots]:
            copy.wait_recv()
        for j in list(range(1, nc)) + [0]:
            for k in range(slots):
                picks[h, ahead(j), k] = parts[h][owner_ref[ahead(j) * slots + k]]
            if j:
                copy = remote(
                    picks.at[h, ahead(j)],
                    chosen.at[h, col * pieces + here],
                    a2_send.at[h, j - 1],
                    a2_recv.at[h, j - 1],
                    {"col": ahead(j)},
                )
                copy.start()
                second.append(copy)
        chosen[h, col * pieces + here] = picks[h, col]

    third, fourth = [], []

    def spread_share(h, j):
        at = chosen.at[h, behind(j) * pieces + here]
        for send, recv, target in (
            (a3x_send.at[h, j], a3x_recv.at[h, j], across),
            (a3c_send.at[h, j], a3c_recv.at[h, j], sibling),
        ):
            copy = remote(at, at, send, recv, target)
            copy.start()
            third.append(copy)

    def forward_share(h, j):
        third[2 * (h * nc + j)].wait_recv()
        at = chosen.at[h, behind(j) * pieces + beside]
        copy = remote(at, at, a3c_send.at[h, nc + j], a3c_recv.at[h, nc + j], sibling)
        copy.start()
        fourth.append(copy)

    mix_part(1)
    for h in range(halves):
        spread_share(h, 0)
        for j in range(1, nc):
            second[h * (nc - 1) + j - 1].wait_recv()
            spread_share(h, j)
    loads[3].wait()
    loads[4].wait()

    lane = lax.broadcasted_iota(jnp.int32, (1, rank_cols), 1)
    sums = []
    for h in range(halves):
        for j in range(nc):
            forward_share(h, j)
        for j in range(nc):
            third[2 * (h * nc + j) + 1].wait_recv()
            fourth[h * nc + j].wait_recv()
        for i in range(rows_here):
            total = jnp.zeros((part, tile), jnp.float32)
            for k in range(slots):
                coeffs = jnp.dot(
                    chosen[h, :, k].reshape(part, tile),
                    right[i, k],
                    preferred_element_type=jnp.float32,
                )
                coeffs = jnp.where(lane < ranks_ref[i, k] * RB, coeffs, 0.0).astype(jnp.bfloat16)
                total += lax.dot_general(
                    coeffs, left[i, k], (((1,), (1,)), ((), ())), preferred_element_type=jnp.float32
                )
            partial_sums[h, :, :, i * tile : (i + 1) * tile] = total.astype(jnp.bfloat16).reshape(
                nc, block, tile
            )
        for j in range(1, nc):
            copy = remote(
                partial_sums.at[h, ahead(j)],
                arrived.at[h, j - 1],
                rs_send.at[h, j - 1],
                rs_recv.at[h, j - 1],
                {"col": ahead(j)},
            )
            copy.start()
            sums.append(copy)
    mix_part(2)

    relayed = []

    def piece(r, b, i):
        return layers.at[r, i, b]

    def pass_on(cond, r, b, i, send, recv, target):
        copy = remote(piece(r, b, i), piece(r, b, i), send, recv, target)
        if cond is None:
            copy.start()
        else:
            pl.when(cond)(copy.start)
        relayed.append((cond, copy))

    def both(x, y):
        return y if x is None else jnp.logical_and(x, y)

    def hand_out(cond, s, up, i):
        b = col - s if up else col + s
        if s < nc - 1:
            for way in (True, False) if s == 0 else (up,):
                n = (s * 2 + way) * halves + i
                more = both(cond, col < nc - 1 if way else col > 0)
                target = {"col": lax.rem(col + (1 if way else nc - 1), nc)}
                pass_on(more, here, b, i, z_send.at[n], z_recv.at[n], target)
        n = (s * 2 + up) * halves + i
        pass_on(cond, here, b, i, x_send.at[n], x_recv.at[n], across)
        pass_on(cond, here, b, i, c_send.at[0, n], c_recv.at[0, n], sibling)

    def await_recv(cond, r, b, i, send, recv):
        copy = remote(piece(r, b, i), piece(r, b, i), send, recv, sibling)
        if cond is None:
            copy.wait_recv()
        else:
            pl.when(cond)(copy.wait_recv)

    def valid(s, up):
        return None if s == 0 else (col >= s if up else col < nc - s)

    def take_z(s, up, i):
        n = ((s - 1) * 2 + up) * halves + i
        b = col - s if up else col + s
        await_recv(valid(s, up), here, b, i, z_send.at[n], z_recv.at[n])
        hand_out(valid(s, up), s, up, i)

    def take_x(s, up, i):
        n = (s * 2 + up) * halves + i
        b = col - s if up else col + s
        await_recv(valid(s, up), beside, b, i, x_send.at[n], x_recv.at[n])
        pass_on(valid(s, up), beside, b, i, c_send.at[1, n], c_recv.at[1, n], sibling)

    def ways(s):
        return (True,) if s == 0 else (True, False)

    for h in range(halves):
        for j in range(1, nc):
            sums[h * (nc - 1) + j - 1].wait_recv()
        total = partial_sums[h, col].astype(jnp.float32)
        for j in range(1, nc):
            total += arrived[h, j - 1].astype(jnp.float32)
        layers[here, h, col] = total.astype(jnp.bfloat16)
        hand_out(None, 0, True, h)
        mix_part(3 + (h == halves - 1))
    for s in range(1, nc):
        for h in range(halves):
            for up in ways(s):
                take_z(s, up, h)
            for up in ways(s - 1):
                take_x(s - 1, up, h)
    other = row * 2 + 1 - core
    other_beside = (1 - row) * 2 + 1 - core
    depth = layers.shape[4]
    for h in range(halves):
        for up in ways(nc - 1):
            take_x(nc - 1, up, h)
        for s in range(nc):
            for up in ways(s):
                n = (s * 2 + up) * halves + h
                b = col - s if up else col + s
                await_recv(valid(s, up), other, b, h, c_send.at[0, n], c_recv.at[0, n])
                await_recv(valid(s, up), other_beside, b, h, c_send.at[1, n], c_recv.at[1, n])
        total = jnp.zeros((part, out_ref.shape[2]), jnp.float32)
        for r in range(pieces):
            total += jnp.dot(
                layers[r, h].reshape(part, depth),
                mixing[r * depth : (r + 1) * depth, :],
                preferred_element_type=jnp.float32,
            )
        out_ref[0, h * part : (h + 1) * part, :] = total.astype(jnp.bfloat16)
    for copy in first + second + third + fourth + sums:
        copy.wait_send()
    for cond, copy in relayed:
        if cond is None:
            copy.wait_send()
        else:
            pl.when(cond)(copy.wait_send)


def fused(
    nc, slopes_in, basis_left, basis_right, rank_blocks, tile_owner, footprint, trace_weight, fitting
):
    frames = slopes_in.shape[0]
    rows_here, slots, tile, rank_cols = basis_left.shape
    pieces = 4
    halves = 2
    part = frames // halves
    share = part // (nc * pieces)
    points = rows_here * tile * pieces
    pupil_count, acts = fitting.shape
    step = tile
    bf16 = jnp.bfloat16
    dma = pltpu.SemaphoreType.DMA
    anywhere = pl.BlockSpec(memory_space=pl.ANY)
    smem = pl.BlockSpec(memory_space=pltpu.SMEM)
    vmem = pl.BlockSpec(memory_space=pltpu.VMEM)
    return pl.pallas_call(
        functools.partial(fused_kernel, nc),
        out_shape=jax.ShapeDtypeStruct((1, frames, acts), bf16),
        in_specs=[smem, smem] + [anywhere] * 6,
        out_specs=vmem,
        scratch_shapes=[
            pltpu.VMEM(footprint.shape, jnp.int32),
            pltpu.VMEM(trace_weight.shape, jnp.float32),
            pltpu.VMEM(basis_left.shape, bf16),
            pltpu.VMEM(basis_right.shape, bf16),
            pltpu.VMEM(fitting.shape, bf16),
            pltpu.VMEM((nc * slots, share, tile), bf16),
            pltpu.VMEM((nc * slots, share, tile), bf16),
            pltpu.VMEM((halves, nc, slots, share, tile), bf16),
            pltpu.VMEM((halves, nc * pieces, slots, share, tile), bf16),
            pltpu.VMEM((step, pupil_count), bf16),
            pltpu.VMEM((points, acts), bf16),
            pltpu.VMEM((halves, nc, part // nc, rows_here * tile), bf16),
            pltpu.VMEM((halves, nc - 1, part // nc, rows_here * tile), bf16),
            pltpu.VMEM((pieces, halves, nc, part // nc, rows_here * tile), bf16),
            dma((5 + halves * slots,)),
            dma((halves, (nc - 1) * slots)),
            dma((halves, (nc - 1) * slots)),
            dma((halves, nc - 1)),
            dma((halves, nc - 1)),
            dma((halves, nc)),
            dma((halves, nc)),
            dma((halves, 2 * nc)),
            dma((halves, 2 * nc)),
            dma((halves, nc - 1)),
            dma((halves, nc - 1)),
            dma((2 * nc * halves,)),
            dma((2 * nc * halves,)),
            dma((2 * nc * halves,)),
            dma((2 * nc * halves,)),
            dma((2, 2 * nc * halves)),
            dma((2, 2 * nc * halves)),
        ],
        compiler_params=pltpu.CompilerParams(
            collective_id=0, has_side_effects=True, vmem_limit_bytes=52 * 2**20
        ),
    )(
        tile_owner,
        rank_blocks,
        slopes_in,
        basis_left,
        basis_right,
        footprint,
        trace_weight,
        fitting,
    )


def solution(mesh):
    placed = (
        P(None, ("grp", "col")),
        P(("row", "dir"), "col", None, None),
        P(("row", "dir"), "col", None, None),
        P(("row", "dir"), "col"),
        P(),
        P(("row", "dir"), None, None, None),
        P(("row", "dir"), None, None, None),
        P(None, "col"),
    )

    def shards(slopes_in, basis_left, basis_right, rank_blocks, tile_owner, footprint, *rest):
        nc = mesh.shape["col"]
        pieces = mesh.shape["row"] * mesh.shape["dir"]
        tile = basis_left.shape[2]
        per_layer = basis_left.shape[0] * pieces * tile // footprint.shape[1]
        fits = (
            mesh.shape["row"] == 2
            and mesh.shape["dir"] == 2
            and nc > 1
            and slopes_in.shape[0] % (2 * nc * pieces * 16) == 0
            and slopes_in.shape[1] == basis_left.shape[1] * tile
            and per_layer % tile == 0
        )
        body = functools.partial(fused, nc) if fits else plain
        return body(
            slopes_in, basis_left, basis_right, rank_blocks, tile_owner, footprint, *rest
        )

    return jax.shard_map(
        shards,
        mesh=mesh,
        in_specs=placed,
        out_specs=P(("row", "dir"), "grp", "col"),
        check_vma=False,
    )
```
